256 devices in a mesh: rep: 8 (over z_lo, core), shard: 32 (over z_hi, y, x).
Axes of the slice: x: 4, y: 4, z: 8 (z_hi: 2, z_lo: 4; z = z_hi * 4 + z_lo), core: 2. Of those that a mesh axis runs over, the one named last changes fastest.
Arguments:
- grad_parts: bfloat16 [8, 32, 128, 5120], P('rep', 'shard'), may hold values from -2 to 2
- momentum: float32 [8, 128, 5120], P('rep', 'shard'), may hold values from -6 to 6
- params: float32 [128, 5120], P('shard'), may hold values from -6 to 6
- indices: int32 [8, 128, 640], P('rep', 'shard'), may hold values from 0 to 63, as said below
Outputs:
- new_momentum: float32 [8, 128, 5120], P('rep', 'shard')
- new_params: float32 [128, 5120], P('shard')
The draws below stay inside these ranges and needn't reach their ends.
Inputs may be any that keep to these rules, and one draw needn't show every extreme that they name: `indices`: the 8 positions of one block and replica are distinct.
All inputs are finite; a program needn't handle non-finite values.
Results may differ from the reference program's by a relative error of at most 0.0003.
Values sent between devices are 32-bit elements; how exact they have to be, the bound alone decides.
A program may use at most 64 MiB of HBM per device.

```python
import math
import jax
import jax.numpy as jnp
from jax import lax

D = 5120
SPAN = 64
KEEP = 8
ROWS = 128
REPS = 8
N_SHARD = 32


def draw_indices(key, part):
    key = jax.random.fold_in(key, 7)
    scores = jax.random.randint(key, (REPS, ROWS, D // SPAN, SPAN), 0, 2 ** 20)
    scores = scores * SPAN + lax.iota(jnp.int32, SPAN)
    chosen = lax.top_k(scores, KEEP)[1]
    return chosen.astype(jnp.int32).reshape(REPS, ROWS, D // 8)


def raised(array, key, source, target, blocks, factor):
    def block_of(dim):
        return (jnp.arange(array.shape[dim]) // (array.shape[dim] // blocks)).reshape((-1,) + (1,) * (array.ndim - 1 - dim))

    near = jax.random.permutation(key, blocks)[block_of(target)]
    second = (block_of(target) + blocks // 2) % blocks
    return jnp.where((block_of(source) == near) | (block_of(source) == second), factor * array, array)


def block_levels(own_key, dims, shards, least, high):
    gain = 1.0
    for axis_at, shards_of in shards:
        heights = jax.random.uniform(jax.random.fold_in(jax.random.fold_in(own_key, 6), axis_at), (shards_of,), jnp.float32, least / len(shards), high / len(shards))
        gain = gain * jnp.repeat(jnp.exp(heights), dims[axis_at] // shards_of).reshape((-1,) + (1,) * (len(dims) - 1 - axis_at))
    return gain


def gaussian(key, shape, deviation, limit, split=(), dtype=jnp.bfloat16):
    result = deviation * jax.random.normal(key, shape, jnp.float32)
    if split:
        result = result * block_levels(key, shape, split, -0.22, 0.18)
    return jnp.clip(result, -limit, limit).astype(dtype)


def bell_draw_with(own_key, shape, width, reach, split, heavy, held_as=jnp.bfloat16):
    entries = width * jax.random.normal(own_key, shape, jnp.float32)
    if split:
        entries = entries * block_levels(own_key, shape, split, -0.22, 0.18)
    return jnp.clip(raised(entries, jax.random.fold_in(own_key, 3), *heavy), -reach, reach).astype(held_as)


def setup_inputs(seed: int = 0) -> dict:
    key_of = jax.random.split(jax.random.key(seed), 5)
    grad_parts = bell_draw_with(key_of[0], (REPS, N_SHARD, ROWS, D), (N_SHARD ** -0.5), 2.0, ((0, 8), (1, 32)), (1, 2, 32, 2.75))
    momentum = gaussian(key_of[1], (REPS, ROWS, D), 1.0, 6.0, ((0, 8), (1, 32)), jnp.float32)
    params = gaussian(key_of[2], (ROWS, D), 1.0, 6.0, ((0, 32),), jnp.float32)
    indices = draw_indices(jax.random.fold_in(key_of[4], 71), 0)
    return dict(grad_parts=grad_parts, momentum=momentum, params=params, indices=indices)


momentum_decay = 0.9
step_size = 1.0

def dct_table():
    freq = lax.iota(jnp.float32, SPAN)[:, None]
    place = lax.iota(jnp.float32, SPAN)[None, :]
    table = jnp.cos(math.pi * (place + 0.5) * freq / SPAN)
    factor = jnp.where(freq == 0.0, math.sqrt(1.0 / SPAN), math.sqrt(2.0 / SPAN))
    return (table * factor).astype(jnp.float32)

def spread(values, picks):
    slots = lax.iota(jnp.int32, SPAN)
    onehot = (picks[..., None] == slots).astype(jnp.float32)
    return lax.optimization_barrier(jnp.sum(values[..., None] * onehot, axis=-2))

def reference(grad_parts, momentum, params, indices):
    forward = dct_table()

    def one_replica(inputs):
        parts, moment, picks = inputs
        gsum = lax.optimization_barrier(jnp.sum(parts.astype(jnp.float32), axis=0))
        blend = momentum_decay * moment + gsum
        blocks = blend.reshape(ROWS, D // SPAN, SPAN)
        coef = jnp.einsum('rcn,kn->rck', blocks, forward, precision=lax.Precision.HIGHEST)
        chosen_at = picks.reshape(ROWS, D // SPAN, KEEP)
        chosen = jnp.take_along_axis(coef, chosen_at, axis=2)
        dense = spread(chosen, chosen_at)
        back = jnp.einsum('rck,kn->rcn', dense, forward, precision=lax.Precision.HIGHEST)
        return (blend - back.reshape(ROWS, D), dense)
    new_momentum, denses = lax.map(one_replica, (grad_parts, momentum, indices))
    average = lax.optimization_barrier(jnp.sum(denses, axis=0)) / REPS
    update = jnp.einsum('rck,kn->rcn', average, forward, precision=lax.Precision.HIGHEST)
    new_params = params - step_size * update.reshape(ROWS, D)
    return (new_momentum, new_params)
```

```python
import functools
import math

import jax
import jax.numpy as jnp
import numpy as np
from jax import lax
from jax.experimental import pallas as pl
from jax.experimental.pallas import tpu as pltpu
from jax.sharding import PartitionSpec as P

SPAN = 64
KEEP = 8
REPS = 8
DECAY = 0.9
LANES = 128
TILES = 8
ROWS4 = 4
BLOCK = TILES * ROWS4
WIDE = TILES * LANES
LAST = 4
CHUNKS = 5
MESH = pl.DeviceIdType.MESH
F32 = jnp.float32


def tables():
    freq = np.arange(SPAN, dtype=np.float64)[:, None]
    place = np.arange(SPAN, dtype=np.float64)[None, :]
    table = np.cos(math.pi * (place + 0.5) * freq / SPAN)
    table = table * np.where(freq == 0.0, math.sqrt(1.0 / SPAN), math.sqrt(2.0 / SPAN))
    pair = np.kron(np.eye(2), table)
    return pair.T.astype(np.float32), pair.astype(np.float32)


def dot(a, b):
    return jnp.dot(a, b, precision=lax.Precision.HIGHEST, preferred_element_type=F32)


def lookup(values, lanes):
    return jnp.take_along_axis(values, lanes, axis=1, mode="promise_in_bounds")


def kernel(
    g_hbm, m_hbm, p_hbm, i_hbm, f_hbm, b_hbm, nm_hbm, np_hbm,
    gb, m_v, p_v, i_v, f_v, b_v, nm_v, np_v, relay,
    stage, zout, rz_last, rf, rd, rs, rf_l, rd_l, rs_l,
    s1, r2, s2, rz, s1_l, r2_l, coef, blend, picks, slots, kept,
    in_sem, out_sem, p1_send, p1_recv, p2_send, p2_recv, z_send, z_recv,
    i_send, i_recv, c_send, c_recv, l_send, l_recv,
):
    rep, shard = lax.axis_index("rep"), lax.axis_index("shard")
    zlo, core = rep // 2, rep % 2
    zhi, y, x = shard // 16, (shard // 4) % 4, shard % 4

    def at(zhi_, y_, x_):
        return (rep, zhi_ * 16 + y_ * 4 + x_)

    def step_x(d):
        return at(zhi, y, (x + d) % 4)

    def step_y(d):
        return at(zhi, (y + d) % 4, x)

    z_partner = at(1 - zhi, y, x)
    core_partner = (zlo * 2 + 1 - core, shard)

    def step_l(d):
        return (((zlo + d) % 4) * 2 + core, shard)

    def swap(c):
        return (core + c) % 2

    def first(c, d):
        s = swap(c)
        return at(zhi, (y + s * d) % 4, (x + (1 - s) * d) % 4)

    def second(c, d):
        s = swap(c)
        return at(zhi, (y + (1 - s) * d) % 4, (x + s * d) % 4)

    def place_a(c):
        return x + swap(c) * (y - x)

    def place_b(c):
        return y + swap(c) * (x - y)

    def remote(src, dst, send, recv, device):
        return pltpu.make_async_remote_copy(
            src_ref=src, dst_ref=dst, send_sem=send, recv_sem=recv,
            device_id=device, device_id_type=MESH,
        )

    sent = []

    def go(copy):
        copy.start()
        sent.append(copy)

    def cols(c):
        return pl.ds(c * WIDE, WIDE)

    loads = {}
    for n, c in enumerate((0, LAST, 1, 2, 3)):
        loads[c] = pltpu.make_async_copy(g_hbm.at[:, cols(c)], gb.at[c], in_sem.at[c])
        loads[c].start()
    small = [
        pltpu.make_async_copy(i_hbm, i_v, in_sem.at[5]),
        pltpu.make_async_copy(m_hbm, m_v, in_sem.at[6]),
        pltpu.make_async_copy(p_hbm, p_v, in_sem.at[7]),
        pltpu.make_async_copy(f_hbm, f_v, in_sem.at[8]),
        pltpu.make_async_copy(b_hbm, b_v, in_sem.at[9]),
    ]
    for copy in small:
        copy.start()

    barrier = pltpu.get_barrier_semaphore()
    peers = [step_x(1), step_x(-1 + 4), step_y(1), step_y(-1 + 4), step_x(2), step_y(2)]
    peers += [z_partner, core_partner] + [step_l(d) for d in (1, 2, 3)]
    for peer in peers:
        pl.semaphore_signal(barrier, inc=1, device_id=peer, device_id_type=MESH)

    upper = lax.broadcasted_iota(jnp.int32, (8, LANES), 0) // 4
    lane = lax.broadcasted_iota(jnp.int32, (8, LANES), 1)
    low_half = upper == 0

    def convert(c):
        loads[c].wait()
        s = swap(c)

        def group(k, carry):
            z_, y_ = k // 4, k % 4
            rows = pl.ds(pl.multiple_of(k * 16, 16), 16)
            for t in range(0, TILES, 2):
                one = gb[c, rows, t * LANES:(t + 1) * LANES].astype(F32)
                two = gb[c, rows, (t + 1) * LANES:(t + 2) * LANES].astype(F32)
                for h in range(2):
                    u, v = one[8 * h:8 * h + 8], two[8 * h:8 * h + 8]
                    for q in range(2):
                        x_ = 2 * h + q
                        if q == 0:
                            piece = jnp.where(low_half, u, pltpu.roll(v, 4, 0))
                        else:
                            piece = jnp.where(low_half, pltpu.roll(u, 4, 0), v)
                        a_, b_ = x_ + s * (y_ - x_), y_ + s * (x_ - y_)
                        stage[c, a_, z_, b_, 4 * t:4 * t + 8, :] = piece
            return carry

        lax.fori_loop(0, 8, group, 0)

    def half(c, q, h):
        if c == LAST:
            return zout.at[q, pl.ds(2 * h, 2)]
        return stage.at[c, q, h]

    def got(c, kind, h):
        if c == LAST:
            return (rf_l, rd_l, rs_l)[kind].at[h]
        return (rf, rd, rs)[kind].at[c, h]

    def p1_copy(c, n, q, h, kind, slot, d):
        return remote(
            half(c, q, h), got(c, kind, slot), p1_send.at[c, n], p1_recv.at[c, n], first(c, d)
        )

    def p1_start(c):
        p = place_a(c)
        up, down, far = (p + 1) % 4, (p + 3) % 4, (p + 2) % 4
        go(p1_copy(c, 0, far, 0, 0, 0, 1))
        go(p1_copy(c, 1, far, 1, 0, 1, 3))
        go(p1_copy(c, 2, up, 1, 1, 1, 1))
        go(p1_copy(c, 3, down, 0, 1, 0, 3))

    def p1_wait(c, n, kind, slot):
        p = place_a(c)
        p1_copy(c, n, p, slot, kind, slot, 1).wait_recv()

    def p1_sum(c):
        p = place_a(c)
        up, down = (p + 1) % 4, (p + 3) % 4
        p1_wait(c, 0, 0, 0)
        half(c, up, 0)[...] += got(c, 0, 0)[...]
        go(p1_copy(c, 4, up, 0, 2, 0, 1))
        p1_wait(c, 1, 0, 1)
        half(c, down, 1)[...] += got(c, 0, 1)[...]
        go(p1_copy(c, 5, down, 1, 2, 1, 3))

    def p2_block(c, q):
        return s1_l.at[q] if c == LAST else s1.at[c, q]

    def p2_got(c, d):
        return r2_l.at[d - 1] if c == LAST else r2.at[c, d - 1]

    def p2_copy(c, q, d):
        return remote(
            p2_block(c, q), p2_got(c, d), p2_send.at[c, d - 1], p2_recv.at[c, d - 1], second(c, d)
        )

    def p1_end(c):
        p = place_a(c)
        p1_wait(c, 3, 1, 0)
        p1_wait(c, 2, 1, 1)
        p1_wait(c, 4, 2, 0)
        p1_wait(c, 5, 2, 1)
        for h in range(2):
            own, direct, summed = half(c, p, h), got(c, 1, h), got(c, 2, h)
            if c == LAST:
                for n in range(2):
                    s1_l[2 * h + n] = own[n] + direct[n] + summed[n]
            else:
                for n in range(4):
                    s1[c, n, h] = own[n] + direct[n] + summed[n]
        q = place_b(c)
        for d in (2, 1, 3):
            go(p2_copy(c, (q + d) % 4, d))

    def z_copy(c):
        return remote(s2.at[c, 1 - zhi], rz.at[c], z_send.at[c], z_recv.at[c], z_partner)

    def p2_end(c):
        q = place_b(c)
        for d in (1, 3, 2):
            p2_copy(c, q, d).wait_recv()
        if c == LAST:
            return s1_l[q] + r2_l[0] + r2_l[1] + r2_l[2]
        s2[c] = s1[c, q] + r2[c, 0] + r2[c, 1] + r2[c, 2]
        go(z_copy(c))

    def zl_copy():
        return remote(zout, rz_last, z_send.at[LAST], z_recv.at[LAST], z_partner)

    def zl_start():
        for a_ in range(4):
            zout[a_] = stage[LAST, a_, 1 - zhi]
        zl_copy().start()

    def zl_end():
        zl_copy().wait()
        for a_ in range(4):
            zout[a_] = stage[LAST, a_, zhi] + rz_last[a_]

    def pair(buf, c):
        return buf.at[c, pl.ds(zlo * 2, 2)]

    def i_core():
        return remote(picks.at[rep], picks.at[rep], i_send.at[0], i_recv.at[0], core_partner)

    def i_pair(d):
        both = picks.at[pl.ds(zlo * 2, 2)]
        return remote(both, both, i_send.at[d], i_recv.at[d], step_l(d))

    def i_start():
        small[0].wait()
        for c in range(CHUNKS):
            four = i_v[:, c * LANES:(c + 1) * LANES]
            picks[rep, c, 0:4, :] = four
            picks[rep, c, 4:8, :] = four
        go(i_core())

    def i_forward():
        i_core().wait_recv()
        for d in (2, 1, 3):
            go(i_pair(d))

    def i_end():
        for d in (1, 2, 3):
            i_pair(d).wait_recv()

    def make_slots(c):
        nothing = 16 - 16 * upper
        base = 16 * upper + 8 * (lane // SPAN)
        want = lane % SPAN

        def one(r, carry):
            have = picks[r, c]
            for v in range(4):
                found = nothing
                for j in range(KEEP):
                    source = base + (32 * v + j)
                    found = jnp.where(lookup(have, source) == want, source, found)
                slots[r, c, v] = found
            return carry

        lax.fori_loop(0, REPS, one, 0)

    def c_core(c):
        return remote(kept.at[c, rep], kept.at[c, rep], c_send.at[c], c_recv.at[c], core_partner)

    def c_pair(c, d):
        both = pair(kept, c)
        return remote(both, both, l_send.at[c, d - 1], l_recv.at[c, d - 1], step_l(d))

    def to_rows(ref, c):
        for t in range(TILES):
            at_ = (c * TILES + t) * LANES
            relay[0, 4 * t:4 * t + 4, :] = ref[:, at_:at_ + LANES]
        return relay[0]

    def from_rows(value, ref, c, n):
        relay[n] = value
        for t in range(TILES):
            at_ = (c * TILES + t) * LANES
            ref[:, at_:at_ + LANES] = relay[n, 4 * t:4 * t + 4, :]

    def transform(c, grad):
        now = DECAY * to_rows(m_v, c) + grad
        blend[c] = now
        out = dot(now, f_v[...])
        coef[c] = out
        places = picks[rep, c] + SPAN * ((lane // KEEP) % 2)
        got_ = jnp.zeros((8, LANES), F32)
        for v in range(4):
            mine = lane // 16 == 2 * v + upper
            got_ = jnp.where(mine, lookup(out[8 * v:8 * v + 8], places), got_)
        kept[c, rep] = got_
        go(c_core(c))

    def z_end(c):
        z_copy(c).wait_recv()
        transform(c, s2[c, zhi] + rz[c])

    def c_forward(c):
        c_core(c).wait_recv()
        for d in (2, 1, 3):
            go(c_pair(c, d))

    outs = []

    def put(ref, hbm, c, n):
        copy = pltpu.make_async_copy(ref.at[:, cols(c)], hbm.at[:, cols(c)], out_sem.at[n, c])
        copy.start()
        outs.append(copy)

    def momentum_out(c):
        mine = kept[c, rep]
        dense = jnp.concatenate([lookup(mine, slots[rep, c, v]) for v in range(4)], axis=0)
        from_rows(blend[c] - dot(dense, b_v[...]), nm_v, c, 1)
        put(nm_v, nm_hbm, c, 0)

    def params_out(c):
        for d in (1, 2, 3):
            c_pair(c, d).wait_recv()
        parts = []
        for v in range(4):
            total = lookup(kept[c, 0], slots[0, c, v])
            for r in range(1, REPS):
                total = total + lookup(kept[c, r], slots[r, c, v])
            parts.append(total)
        average = jnp.concatenate(parts, axis=0) / REPS
        from_rows(to_rows(p_v, c) - dot(average, b_v[...]), np_v, c, 2)
        put(np_v, np_hbm, c, 1)

    convert(0)
    pl.semaphore_wait(barrier, len(peers))
    p1_start(0)
    convert(LAST)
    zl_start()
    convert(1)
    p1_start(1)
    i_start()
    p1_sum(0)
    convert(2)
    p1_start(2)
    i_forward()
    p1_end(0)
    p1_sum(1)
    convert(3)
    p1_start(3)
    for copy in small[1:]:
        copy.wait()
    i_end()
    make_slots(0)
    p2_end(0)
    p1_end(1)
    p1_sum(2)
    make_slots(1)
    zl_end()
    p1_start(LAST)
    p2_end(1)
    make_slots(2)
    p1_end(2)
    p1_sum(3)
    z_end(0)
    make_slots(3)
    make_slots(4)
    p2_end(2)
    p1_sum(LAST)
    c_forward(0)
    momentum_out(0)
    p1_end(3)
    z_end(1)
    p1_end(LAST)
    c_forward(1)
    p2_end(3)
    momentum_out(1)
    z_end(2)
    grad_last = p2_end(LAST)
    transform(LAST, grad_last)
    c_forward(2)
    params_out(0)
    c_forward(LAST)
    z_end(3)
    params_out(1)
    c_forward(3)
    momentum_out(2)
    momentum_out(LAST)
    momentum_out(3)
    params_out(2)
    params_out(LAST)
    params_out(3)
    for copy in sent:
        copy.wait_send()
    for copy in outs:
        copy.wait()


def local(grad_parts, momentum, params, indices):
    forward, back = tables()
    any_ = pl.BlockSpec(memory_space=pl.ANY)
    vmem = pltpu.VMEM
    dma = pltpu.SemaphoreType.DMA
    n = CHUNKS - 1
    block = (BLOCK, LANES)
    new_momentum, new_params = pl.pallas_call(
        kernel,
        out_shape=(
            jax.ShapeDtypeStruct(momentum.shape[1:], F32),
            jax.ShapeDtypeStruct(params.shape, F32),
        ),
        in_specs=[any_] * 6,
        out_specs=(any_, any_),
        scratch_shapes=[
            vmem((CHUNKS, 128, WIDE), jnp.bfloat16),
            vmem(params.shape, F32),
            vmem(params.shape, F32),
            vmem(indices.shape[1:], jnp.int32),
            vmem((LANES, LANES), F32),
            vmem((LANES, LANES), F32),
            vmem(params.shape, F32),
            vmem(params.shape, F32),
            vmem((3, *block), F32),
            vmem((CHUNKS, 4, 2, 4, *block), F32),
            vmem((4, 4, *block), F32),
            vmem((4, 4, *block), F32),
            vmem((n, 2, 4, *block), F32),
            vmem((n, 2, 4, *block), F32),
            vmem((n, 2, 4, *block), F32),
            vmem((2, 2, *block), F32),
            vmem((2, 2, *block), F32),
            vmem((2, 2, *block), F32),
            vmem((n, 4, 2, *block), F32),
            vmem((n, 3, 2, *block), F32),
            vmem((n, 2, *block), F32),
            vmem((n, *block), F32),
            vmem((4, *block), F32),
            vmem((3, *block), F32),
            vmem((CHUNKS, *block), F32),
            vmem((CHUNKS, *block), F32),
            vmem((REPS, CHUNKS, 8, LANES), jnp.int32),
            vmem((REPS, CHUNKS, 4, 8, LANES), jnp.int32),
            vmem((CHUNKS, REPS, 8, LANES), F32),
            dma((10,)),
            dma((2, CHUNKS)),
            dma((CHUNKS, 6)),
            dma((CHUNKS, 6)),
            dma((CHUNKS, 3)),
            dma((CHUNKS, 3)),
            dma((CHUNKS,)),
            dma((CHUNKS,)),
            dma((4,)),
            dma((4,)),
            dma((CHUNKS,)),
            dma((CHUNKS,)),
            dma((CHUNKS, 3)),
            dma((CHUNKS, 3)),
        ],
        compiler_params=pltpu.CompilerParams(
            collective_id=0, has_side_effects=True, vmem_limit_bytes=40 << 20
        ),
        name="step",
    )(grad_parts[0, 0], momentum[0], params, indices[0], forward, back)
    return new_momentum[None], new_params


def solution(mesh):
    in_specs = (
        P("rep", "shard", None, None),
        P("rep", "shard", None),
        P("shard", None),
        P("rep", "shard", None),
    )
    out_specs = (P("rep", "shard", None), P("shard", None))
    return jax.shard_map(local, mesh=mesh, in_specs=in_specs, out_specs=out_specs, check_vma=False)
```

```python
import functools
import math

import jax
import jax.numpy as jnp
import numpy as np
from jax import lax
from jax.experimental import pallas as pl
from jax.experimental.pallas import tpu as pltpu
from jax.sharding import PartitionSpec as P

SPAN = 64
KEEP = 8
REPS = 8
DECAY = 0.9
LANES = 128
TILES = 8
BLOCK = 4 * TILES
WIDE = TILES * LANES
CHUNKS = ((0, 2, 0), (2, 2, 1), (4, 1, 0))
INDEX_TILES = 5
MESH = pl.DeviceIdType.MESH
F32 = jnp.float32


def tables():
    freq = np.arange(SPAN, dtype=np.float64)[:, None]
    place = np.arange(SPAN, dtype=np.float64)[None, :]
    table = np.cos(math.pi * (place + 0.5) * freq / SPAN)
    table = table * np.where(freq == 0.0, math.sqrt(1.0 / SPAN), math.sqrt(2.0 / SPAN))
    pair = np.kron(np.eye(2), table)
    return pair.T.astype(np.float32), pair.astype(np.float32)


def dot(a, b):
    return jnp.dot(a, b, precision=lax.Precision.HIGHEST, preferred_element_type=F32)


def lookup(values, lanes):
    return jnp.take_along_axis(values, lanes, axis=1, mode="promise_in_bounds")


def kernel(names, *refs):
    r_ = dict(zip(names, refs))
    rep, shard = lax.axis_index("rep"), lax.axis_index("shard")
    zlo, core = rep // 2, rep % 2
    zhi, y, x = shard // 16, (shard // 4) % 4, shard % 4

    def at(zhi_, y_, x_):
        return (rep, zhi_ * 16 + y_ * 4 + x_)

    def step_x(d):
        return at(zhi, y, (x + d) % 4)

    def step_y(d):
        return at(zhi, (y + d) % 4, x)

    core_partner = (zlo * 2 + 1 - core, shard)

    def step_l(d, far=0):
        half_ = zhi + far * (1 - 2 * zhi)
        return (((zlo + d) % 4) * 2 + core, half_ * 16 + y * 4 + x)

    def swap(c):
        return (core + CHUNKS[c][2]) % 2

    def first(c, d):
        s = swap(c)
        return at(zhi, (y + s * d) % 4, (x + (1 - s) * d) % 4)

    def second(c, d):
        s = swap(c)
        return at(zhi, (y + (1 - s) * d) % 4, (x + s * d) % 4)

    def place_a(c):
        return x + swap(c) * (y - x)

    def place_b(c):
        return y + swap(c) * (x - y)

    def buf(name, c):
        return r_[name + str(c)]

    def sems(name, c, n):
        return r_[name + "_send"].at[c, n], r_[name + "_recv"].at[c, n]

    def remote(src, dst, pair, device):
        return pltpu.make_async_remote_copy(
            src_ref=src, dst_ref=dst, send_sem=pair[0], recv_sem=pair[1],
            device_id=device, device_id_type=MESH,
        )

    sent = []

    def go(copy):
        copy.start()
        sent.append(copy)

    def flush():
        while sent:
            sent.pop(0).wait_send()

    loads = []
    for c, (tile, count, _) in enumerate(CHUNKS):
        loads.append(
            pltpu.make_async_copy(
                r_["g_hbm"].at[:, pl.ds(tile * WIDE, count * WIDE)], buf("gb", c), r_["in_sem"].at[c]
            )
        )
    small = [
        pltpu.make_async_copy(r_[a], r_[b], r_["in_sem"].at[len(CHUNKS) + n])
        for n, (a, b) in enumerate(
            (("i_hbm", "i_v"), ("m_hbm", "m_v"), ("p_hbm", "p_v"), ("f_hbm", "f_v"), ("b_hbm", "b_v"))
        )
    ]
    for copy in loads[:1] + small[:1] + loads[1:] + small[1:]:
        copy.start()

    barrier = pltpu.get_barrier_semaphore()
    peers = [step_x(1), step_x(3), step_y(1), step_y(3), step_x(2), step_y(2)]
    peers += [core_partner] + [step_l(d) for d in (1, 2, 3)] + [step_l(d, 1) for d in range(4)]
    for peer in peers:
        pl.semaphore_signal(barrier, inc=1, device_id=peer, device_id_type=MESH)

    upper = lax.broadcasted_iota(jnp.int32, (8, LANES), 0) // 4
    lane = lax.broadcasted_iota(jnp.int32, (8, LANES), 1)
    low_half = upper == 0

    def convert(c, z_):
        s = swap(c)
        gb, stage = buf("gb", c), buf("stage", c)

        def group(y_, carry):
            rows = pl.ds(pl.multiple_of(z_ * 64 + y_ * 16, 16), 16)
            for t in range(0, CHUNKS[c][1] * TILES, 2):
                one = gb[rows, t * LANES:(t + 1) * LANES].astype(F32)
                two = gb[rows, (t + 1) * LANES:(t + 2) * LANES].astype(F32)
                for h in range(2):
                    u, v = one[8 * h:8 * h + 8], two[8 * h:8 * h + 8]
                    for q in range(2):
                        x_ = 2 * h + q
                        if q == 0:
                            piece = jnp.where(low_half, u, pltpu.roll(v, 4, 0))
                        else:
                            piece = jnp.where(low_half, pltpu.roll(u, 4, 0), v)
                        a_, b_ = x_ + s * (y_ - x_), y_ + s * (x_ - y_)
                        stage[a_, z_, b_, 4 * t:4 * t + 8, :] = piece
            return carry

        lax.fori_loop(0, 4, group, 0)

    def half(c, q, h):
        return buf("stage", c).at[q, h]

    def got(c, kind, h):
        return buf(("rf", "rd", "rs")[kind], c).at[h]

    def p1_copy(c, n, q, h, kind, slot, d):
        return remote(half(c, q, h), got(c, kind, slot), sems("p1", c, n), first(c, d))

    def p1_forward(c):
        far = (place_a(c) + 2) % 4
        go(p1_copy(c, 0, far, 0, 0, 0, 1))
        go(p1_copy(c, 1, far, 1, 0, 1, 3))

    def p1_direct(c):
        p = place_a(c)
        go(p1_copy(c, 2, (p + 1) % 4, 1, 1, 1, 1))
        go(p1_copy(c, 3, (p + 3) % 4, 0, 1, 0, 3))

    def p1_wait(c, n, kind, slot):
        p1_copy(c, n, place_a(c), slot, kind, slot, 1).wait_recv()

    def p1_sum(c):
        p = place_a(c)
        up, down = (p + 1) % 4, (p + 3) % 4
        p1_wait(c, 0, 0, 0)
        half(c, up, 0)[...] += got(c, 0, 0)[...]
        go(p1_copy(c, 4, up, 0, 2, 0, 1))
        p1_wait(c, 1, 0, 1)
        half(c, down, 1)[...] += got(c, 0, 1)[...]
        go(p1_copy(c, 5, down, 1, 2, 1, 3))

    def p2_copy(c, q, d):
        return remote(buf("s1", c).at[q], buf("r2", c).at[d - 1], sems("p2", c, d - 1), second(c, d))

    def p1_end(c):
        p, s1 = place_a(c), buf("s1", c)
        for n, kind, slot in ((3, 1, 0), (2, 1, 1), (4, 2, 0), (5, 2, 1)):
            p1_wait(c, n, kind, slot)
        for h in range(2):
            own, direct, summed = half(c, p, h), got(c, 1, h), got(c, 2, h)
            for n in range(4):
                s1[n, h] = own[n] + direct[n] + summed[n]
        q = place_b(c)
        for d in (2, 1, 3):
            go(p2_copy(c, (q + d) % 4, d))

    def z_copy(c):
        return remote(buf("s2", c).at[1 - zhi], buf("rz", c), sems("z", c, 0), step_l(0, 1))

    def p2_end(c):
        q, r2 = place_b(c), buf("r2", c)
        for d in (1, 3, 2):
            p2_copy(c, q, d).wait_recv()
        buf("s2", c)[...] = buf("s1", c)[q] + r2[0] + r2[1] + r2[2]

    def pick_copy(d):
        mine = r_["picks"].at[core, zlo]
        return remote(mine, mine, sems("pick", 0, d), step_l(d))

    def pick_far():
        return remote(r_["picks"].at[core, zlo], r_["far_picks"], sems("pick", 0, 4), step_l(0, 1))

    def core_copy(ref, name, n):
        return remote(ref.at[core], ref.at[core], sems(name, 0, n), core_partner)

    def kept_copy(c, d, far):
        source = r_["far_kept"].at[c] if far else r_["kept"].at[0, zlo, c]
        n = 3 + d if far else d - 1
        return remote(source, r_["kept"].at[far, zlo, c], sems("kept", c, n), step_l(d, far))

    ways = ((0, 1), (2, 0), (1, 1), (3, 1), (1, 0), (3, 0), (2, 1))

    def kept_end(c):
        for d, far in ways:
            kept_copy(c, d, far).wait_recv()

    picks, slots, spots, kept, kept_sum = r_["picks"], r_["slots"], r_["spots"], r_["kept"], r_["kept_sum"]

    def i_start():
        small[0].wait()
        for t in range(INDEX_TILES):
            picks[core, zlo, t] = r_["i_v"][:, t * LANES:(t + 1) * LANES]
        for d in (2, 1, 3):
            go(pick_copy(d))
        go(pick_far())

    def i_middle():
        for d in (1, 3, 2):
            pick_copy(d).wait_recv()
        go(core_copy(picks, "pick", 0))
        pick_far().wait_recv()

    def doubled(four):
        return jnp.concatenate([four, pltpu.roll(four, LANES - 16, 1)], axis=0)

    def make_slots():
        rows = INDEX_TILES * REPS * 8
        for t in range(INDEX_TILES):
            for r in range(REPS):
                at_ = (t * REPS + r) * 8
                spots[at_:at_ + 8, :] = doubled(picks[r // 4, r % 4, t]).astype(F32)
        from_row = lax.broadcasted_iota(jnp.int32, (LANES, 2 * LANES), 0)
        column = lax.broadcasted_iota(jnp.int32, (LANES, 2 * LANES), 1)
        to_lane = column % LANES
        wide = lax.broadcasted_iota(jnp.int32, (rows, LANES), 1)
        want = (wide % SPAN).astype(F32)
        tile_of = lax.broadcasted_iota(jnp.int32, (rows, LANES), 0) // (REPS * 8)
        base = KEEP * (wide // SPAN) + 16 * (tile_of % 2)
        have = spots[...].astype(jnp.bfloat16)

        def one(v, carry):
            found = jnp.full((rows, LANES), -1, jnp.int32)
            for j in range(0, KEEP, 2):
                source = 32 * v + KEEP * (to_lane // SPAN) + j + column // LANES
                pick = (from_row == source).astype(F32).astype(jnp.bfloat16)
                spread = jnp.dot(have, pick, preferred_element_type=F32)
                for k in range(2):
                    here = spread[:, k * LANES:(k + 1) * LANES] == want
                    found = jnp.where(here, base + (32 * v + j + k), found)
            slots[v] = found
            return carry

        lax.fori_loop(0, 4, one, 0)

    def slot(v, t, core_, z_):
        at_ = (t * REPS + core_ * 4 + z_) * 8
        return slots[v, pl.ds(pl.multiple_of(at_, 8), 8), :]

    def spread(values, where):
        return jnp.where(where >= 0, lookup(values, jnp.maximum(where, 0)), 0.0)

    def to_rows(ref, out):
        for t in range(INDEX_TILES * TILES):
            out[4 * t:4 * t + 4, :] = ref[:, t * LANES:(t + 1) * LANES]

    def from_rows(value, relay, ref, c):
        tile, count = CHUNKS[c][:2]
        relay[0:count * BLOCK, :] = value
        for t in range(count * TILES):
            at_ = (tile * TILES + t) * LANES
            ref[:, at_:at_ + LANES] = relay[4 * t:4 * t + 4, :]

    def rows_of(c):
        tile, count = CHUNKS[c][:2]
        return slice(tile * BLOCK, (tile + count) * BLOCK)

    def choose(out, positions, c):
        found = jnp.zeros((8, LANES), F32)
        for t in range(CHUNKS[c][1]):
            places = doubled(positions[t])
            if t % 2:
                places = pltpu.roll(places, 16, 1)
            places = places + SPAN * ((lane // KEEP) % 2)
            for v in range(4):
                mine = lane // 16 == 2 * v + t % 2
                part = out[t * BLOCK + 8 * v:t * BLOCK + 8 * v + 8]
                found = jnp.where(mine, lookup(part, places), found)
        return found

    def transform(c):
        tile, count = CHUNKS[c][:2]
        s2 = buf("s2", c)
        own = DECAY * r_["m_rows"][rows_of(c), :] + s2[zhi]
        r_["blend"][rows_of(c), :] = own
        out = dot(jnp.concatenate([own, s2[1 - zhi]], axis=0), r_["f_v"][...])
        rows = count * BLOCK
        kept[0, zlo, c] = choose(out[:rows], [picks[core, zlo, tile + t] for t in range(count)], c)
        r_["far_kept"][c] = choose(out[rows:], [r_["far_picks"][tile + t] for t in range(count)], c)
        for d, far in ways:
            go(kept_copy(c, d, far))
        go(z_copy(c))

    def momentum_out(c):
        tile, count = CHUNKS[c][:2]
        z_copy(c).wait_recv()
        now = r_["blend"][rows_of(c), :] + buf("rz", c)[...]
        own = [slot(v, t, core, zlo) for t in range(tile, tile + count) for v in range(4)]
        dense = jnp.where(jnp.concatenate(own, axis=0) >= 0, dot(now, r_["f_v"][...]), 0.0)
        from_rows(now - dot(dense, r_["b_v"][...]), r_["relay0"], r_["nm_out"], c)

    def core_sum(core_):
        parts = []
        for t in range(INDEX_TILES):
            for v in range(4):
                total = spread(kept_sum[core_, 0, t // 2], slot(v, t, core_, 0))
                for z_ in range(1, 4):
                    total = total + spread(kept_sum[core_, z_, t // 2], slot(v, t, core_, z_))
                parts.append(total)
        return jnp.concatenate(parts, axis=0)

    def params_out():
        for c in range(len(CHUNKS)):
            kept_end(c)
        kept_sum[core] = kept[0] + kept[1]
        copy = core_copy(kept_sum, "pick", 5)
        go(copy)
        r_["relay1"][...] = core_sum(core)
        momentum_out(2)
        copy.wait_recv()
        average = (r_["relay1"][...] + core_sum(1 - core)) / REPS
        r_["relay1"][...] = r_["p_rows"][...] - dot(average, r_["b_v"][...])
        for t in range(INDEX_TILES * TILES):
            r_["np_out"][:, t * LANES:(t + 1) * LANES] = r_["relay1"][4 * t:4 * t + 4, :]

    loads[0].wait()
    convert(0, 0)
    convert(0, 1)
    pl.semaphore_wait(barrier, len(peers))
    p1_forward(0)
    p1_direct(0)
    loads[1].wait()
    convert(1, 0)
    convert(1, 1)
    p1_forward(1)
    i_start()
    loads[2].wait()
    convert(2, 0)
    convert(2, 1)
    p1_sum(0)
    p1_direct(1)
    p1_forward(2)
    for copy in small[1:]:
        copy.wait()
    to_rows(r_["m_v"], r_["m_rows"])
    to_rows(r_["p_v"], r_["p_rows"])
    p1_sum(1)
    p1_direct(2)
    i_middle()
    p1_end(0)
    p1_sum(2)
    p1_end(1)
    p2_end(0)
    transform(0)
    p1_end(2)
    p2_end(1)
    transform(1)
    p2_end(2)
    transform(2)
    core_copy(picks, "pick", 0).wait_recv()
    make_slots()
    flush()
    momentum_out(0)
    momentum_out(1)
    params_out()
    flush()


def scratches(shape):
    vmem, dma = pltpu.VMEM, pltpu.SemaphoreType.DMA
    made = {
        "m_v": vmem(shape, F32),
        "p_v": vmem(shape, F32),
        "i_v": vmem((4, INDEX_TILES * LANES), jnp.int32),
        "f_v": vmem((LANES, LANES), F32),
        "b_v": vmem((LANES, LANES), F32),
        "m_rows": vmem((INDEX_TILES * BLOCK, LANES), F32),
        "p_rows": vmem((INDEX_TILES * BLOCK, LANES), F32),
        "blend": vmem((INDEX_TILES * BLOCK, LANES), F32),
        "relay0": vmem((INDEX_TILES * BLOCK, LANES), F32),
        "relay1": vmem((INDEX_TILES * BLOCK, LANES), F32),
        "picks": vmem((2, 4, INDEX_TILES, 4, LANES), jnp.int32),
        "slots": vmem((4, INDEX_TILES * REPS * 8, LANES), jnp.int32),
        "kept": vmem((2, 4, len(CHUNKS), 8, LANES), F32),
        "kept_sum": vmem((2, 4, len(CHUNKS), 8, LANES), F32),
        "far_kept": vmem((len(CHUNKS), 8, LANES), F32),
        "far_picks": vmem((INDEX_TILES, 4, LANES), jnp.int32),
        "spots": vmem((INDEX_TILES * REPS * 8, LANES), F32),
    }
    for c, (_, count, _) in enumerate(CHUNKS):
        block = (count * BLOCK, LANES)
        made["gb" + str(c)] = vmem((128, count * WIDE), jnp.bfloat16)
        made["stage" + str(c)] = vmem((4, 2, 4, *block), F32)
        for name in ("rf", "rd", "rs"):
            made[name + str(c)] = vmem((2, 4, *block), F32)
        made["s1" + str(c)] = vmem((4, 2, *block), F32)
        made["r2" + str(c)] = vmem((3, 2, *block), F32)
        made["s2" + str(c)] = vmem((2, *block), F32)
        made["rz" + str(c)] = vmem(block, F32)
    made["in_sem"] = dma((len(CHUNKS) + 5,))
    for name, count in (("p1", 6), ("p2", 3), ("z", 1), ("pick", 6), ("kept", 7)):
        for end in ("_send", "_recv"):
            made[name + end] = dma((len(CHUNKS), count))
    return made


def local(grad_parts, momentum, params, indices):
    forward, back = tables()
    hbm = pl.BlockSpec(memory_space=pltpu.HBM)
    vmem = pl.BlockSpec(memory_space=pltpu.VMEM)
    made = scratches(params.shape)
    names = ("g_hbm", "m_hbm", "p_hbm", "i_hbm", "f_hbm", "b_hbm", "nm_out", "np_out", *made)
    operands = (grad_parts[0, 0], momentum[0], params, indices[0], jnp.asarray(forward), jnp.asarray(back))
    new_momentum, new_params = pl.pallas_call(
        functools.partial(kernel, names),
        out_shape=(pltpu.VMEM(params.shape, F32),) * 2,
        in_specs=[hbm] * 6,
        out_specs=(vmem, vmem),
        scratch_shapes=list(made.values()),
        compiler_params=pltpu.CompilerParams(
            collective_id=0, has_side_effects=True, vmem_limit_bytes=60 << 20
        ),
        name="step",
    )(*(pltpu.with_memory_space_constraint(v, pltpu.HBM) for v in operands))
    return new_momentum[None], new_params


def solution(mesh):
    in_specs = (
        P("rep", "shard", None, None),
        P("rep", "shard", None),
        P("shard", None),
        P("rep", "shard", None),
    )
    out_specs = (P("rep", "shard", None), P("shard", None))
    return jax.shard_map(local, mesh=mesh, in_specs=in_specs, out_specs=out_specs, check_vma=False)
```

```python
import functools
import math

import jax
import jax.numpy as jnp
import numpy as np
from jax import lax
from jax.experimental import pallas as pl
from jax.experimental.pallas import tpu as pltpu
from jax.sharding import PartitionSpec as P

SPAN = 64
KEEP = 8
REPS = 8
DECAY = 0.9
LANES = 128
TILES = 8
BLOCK = 4 * TILES
WIDE = TILES * LANES
CHUNKS = ((0, 2, 0), (2, 2, 1), (4, 1, 0))
INDEX_TILES = 5
MESH = pl.DeviceIdType.MESH
F32 = jnp.float32


def tables():
    freq = np.arange(SPAN, dtype=np.float64)[:, None]
    place = np.arange(SPAN, dtype=np.float64)[None, :]
    table = np.cos(math.pi * (place + 0.5) * freq / SPAN)
    table = table * np.where(freq == 0.0, math.sqrt(1.0 / SPAN), math.sqrt(2.0 / SPAN))
    pair = np.kron(np.eye(2), table)
    return pair.T.astype(np.float32), pair.astype(np.float32)


def dot(a, b):
    return jnp.dot(a, b, precision=lax.Precision.HIGHEST, preferred_element_type=F32)


def lookup(values, lanes):
    return jnp.take_along_axis(values, lanes, axis=1, mode="promise_in_bounds")


def kernel(names, *refs):
    r_ = dict(zip(names, refs))
    rep, shard = lax.axis_index("rep"), lax.axis_index("shard")
    zlo, core = rep // 2, rep % 2
    zhi, y, x = shard // 16, (shard // 4) % 4, shard % 4

    def at(zhi_, y_, x_):
        return (rep, zhi_ * 16 + y_ * 4 + x_)

    def step_x(d):
        return at(zhi, y, (x + d) % 4)

    def step_y(d):
        return at(zhi, (y + d) % 4, x)

    core_partner = (zlo * 2 + 1 - core, shard)

    def step_l(d, far=0):
        half_ = zhi + far * (1 - 2 * zhi)
        return (((zlo + d) % 4) * 2 + core, half_ * 16 + y * 4 + x)

    def swap(c):
        return (core + CHUNKS[c][2]) % 2

    def first(c, d):
        s = swap(c)
        return at(zhi, (y + s * d) % 4, (x + (1 - s) * d) % 4)

    def second(c, d):
        s = swap(c)
        return at(zhi, (y + (1 - s) * d) % 4, (x + s * d) % 4)

    def place_a(c):
        return x + swap(c) * (y - x)

    def place_b(c):
        return y + swap(c) * (x - y)

    def buf(name, c):
        return r_[name + str(c)]

    def sems(name, c, n):
        return r_[name + "_send"].at[c, n], r_[name + "_recv"].at[c, n]

    def remote(src, dst, pair, device):
        return pltpu.make_async_remote_copy(
            src_ref=src, dst_ref=dst, send_sem=pair[0], recv_sem=pair[1],
            device_id=device, device_id_type=MESH,
        )

    sent = []

    def go(copy):
        copy.start()
        sent.append(copy)

    def flush(count=None):
        for copy in sent[:count]:
            copy.wait_send()
        del sent[:count]

    loads = []
    for c, (tile, count, _) in enumerate(CHUNKS):
        loads.append(
            pltpu.make_async_copy(
                r_["g_hbm"].at[:, pl.ds(tile * WIDE, count * WIDE)], buf("gb", c), r_["in_sem"].at[c]
            )
        )
    small = [
        pltpu.make_async_copy(r_[a], r_[b], r_["in_sem"].at[len(CHUNKS) + n])
        for n, (a, b) in enumerate(
            (("i_hbm", "i_v"), ("m_hbm", "m_v"), ("p_hbm", "p_v"), ("f_hbm", "f_v"), ("b_hbm", "b_v"))
        )
    ]
    for copy in loads[:1] + small[:1] + loads[1:] + small[1:]:
        copy.start()

    barrier = pltpu.get_barrier_semaphore()
    peers = [step_x(1), step_x(3), step_y(1), step_y(3), step_x(2), step_y(2)]
    peers += [core_partner] + [step_l(d) for d in (1, 2, 3)] + [step_l(d, 1) for d in range(4)]
    for peer in peers:
        pl.semaphore_signal(barrier, inc=1, device_id=peer, device_id_type=MESH)

    upper = lax.broadcasted_iota(jnp.int32, (8, LANES), 0) // 4
    lane = lax.broadcasted_iota(jnp.int32, (8, LANES), 1)
    low_half = upper == 0

    def convert(c, z_):
        s = swap(c)
        gb, stage = buf("gb", c), buf("stage", c)

        def group(y_, carry):
            rows = pl.ds(pl.multiple_of(z_ * 64 + y_ * 16, 16), 16)
            for t in range(0, CHUNKS[c][1] * TILES, 2):
                one = gb[rows, t * LANES:(t + 1) * LANES].astype(F32)
                two = gb[rows, (t + 1) * LANES:(t + 2) * LANES].astype(F32)
                for h in range(2):
                    u, v = one[8 * h:8 * h + 8], two[8 * h:8 * h + 8]
                    for q in range(2):
                        x_ = 2 * h + q
                        if q == 0:
                            piece = jnp.where(low_half, u, pltpu.roll(v, 4, 0))
                        else:
                            piece = jnp.where(low_half, pltpu.roll(u, 4, 0), v)
                        a_, b_ = x_ + s * (y_ - x_), y_ + s * (x_ - y_)
                        stage[a_, z_, b_, 4 * t:4 * t + 8, :] = piece
            return carry

        lax.fori_loop(0, 4, group, 0)

    def half(c, q, h):
        return buf("stage", c).at[q, h]

    def got(c, kind, h):
        return buf(("rf", "rd", "rs")[kind], c).at[h]

    def p1_copy(c, n, q, h, kind, slot, d):
        return remote(half(c, q, h), got(c, kind, slot), sems("p1", c, n), first(c, d))

    def p1_forward(c):
        far = (place_a(c) + 2) % 4
        go(p1_copy(c, 0, far, 0, 0, 0, 1))
        go(p1_copy(c, 1, far, 1, 0, 1, 3))

    def p1_direct(c):
        p = place_a(c)
        go(p1_copy(c, 2, (p + 1) % 4, 1, 1, 1, 1))
        go(p1_copy(c, 3, (p + 3) % 4, 0, 1, 0, 3))

    def p1_wait(c, n, kind, slot):
        p1_copy(c, n, place_a(c), slot, kind, slot, 1).wait_recv()

    def p1_sum(c):
        p = place_a(c)
        up, down = (p + 1) % 4, (p + 3) % 4
        p1_wait(c, 0, 0, 0)
        half(c, up, 0)[...] += got(c, 0, 0)[...]
        go(p1_copy(c, 4, up, 0, 2, 0, 1))
        p1_wait(c, 1, 0, 1)
        half(c, down, 1)[...] += got(c, 0, 1)[...]
        go(p1_copy(c, 5, down, 1, 2, 1, 3))

    def p2_copy(c, q, d):
        return remote(buf("s1", c).at[q], buf("r2", c).at[d - 1], sems("p2", c, d - 1), second(c, d))

    def p1_end(c):
        p, s1 = place_a(c), buf("s1", c)
        for n, kind, slot in ((3, 1, 0), (2, 1, 1), (4, 2, 0), (5, 2, 1)):
            p1_wait(c, n, kind, slot)
        for h in range(2):
            own, direct, summed = half(c, p, h), got(c, 1, h), got(c, 2, h)
            for n in range(4):
                s1[n, h] = own[n] + direct[n] + summed[n]
        q = place_b(c)
        for d in (2, 1, 3):
            go(p2_copy(c, (q + d) % 4, d))

    def z_copy(c):
        return remote(buf("s2", c).at[1 - zhi], buf("rz", c), sems("z", c, 0), step_l(0, 1))

    def p2_end(c):
        q, r2 = place_b(c), buf("r2", c)
        for d in (1, 3, 2):
            p2_copy(c, q, d).wait_recv()
        buf("s2", c)[...] = buf("s1", c)[q] + r2[0] + r2[1] + r2[2]

    def pick_copy(d):
        mine = r_["picks"].at[core, zlo]
        return remote(mine, mine, sems("pick", 0, d), step_l(d))

    def pick_far():
        return remote(r_["picks"].at[core, zlo], r_["far_picks"], sems("pick", 0, 4), step_l(0, 1))

    def core_copy(ref, name, n):
        return remote(ref.at[core], ref.at[core], sems(name, 0, n), core_partner)

    def kept_copy(c, d, far):
        source = r_["far_kept"].at[c] if far else r_["kept"].at[0, zlo, c]
        n = 3 + d if far else d - 1
        return remote(source, r_["kept"].at[far, zlo, c], sems("kept", c, n), step_l(d, far))

    ways = ((0, 1), (2, 0), (1, 1), (3, 1), (1, 0), (3, 0), (2, 1))

    def kept_end(c):
        for d, far in ways:
            kept_copy(c, d, far).wait_recv()

    picks, slots, spots, kept, kept_sum = r_["picks"], r_["slots"], r_["spots"], r_["kept"], r_["kept_sum"]

    def i_start():
        small[0].wait()
        for t in range(INDEX_TILES):
            picks[core, zlo, t] = r_["i_v"][:, t * LANES:(t + 1) * LANES]
        for d in (2, 1, 3):
            go(pick_copy(d))
        go(pick_far())

    def i_middle():
        for d in (1, 3, 2):
            pick_copy(d).wait_recv()
        go(core_copy(picks, "pick", 0))
        pick_far().wait_recv()

    def doubled(four):
        return jnp.concatenate([four, pltpu.roll(four, LANES - 16, 1)], axis=0)

    def make_slots():
        rows = INDEX_TILES * REPS * 8
        for t in range(INDEX_TILES):
            for r in range(REPS):
                at_ = (t * REPS + r) * 8
                spots[at_:at_ + 8, :] = doubled(picks[r // 4, r % 4, t]).astype(F32)
        from_row = lax.broadcasted_iota(jnp.int32, (LANES, 2 * LANES), 0)
        column = lax.broadcasted_iota(jnp.int32, (LANES, 2 * LANES), 1)
        to_lane = column % LANES
        wide = lax.broadcasted_iota(jnp.int32, (rows, LANES), 1)
        want = (wide % SPAN).astype(F32)
        tile_of = lax.broadcasted_iota(jnp.int32, (rows, LANES), 0) // (REPS * 8)
        base = KEEP * (wide // SPAN) + 16 * (tile_of % 2)
        have = spots[...].astype(jnp.bfloat16)

        def one(v, carry):
            found = jnp.full((rows, LANES), -1, jnp.int32)
            for j in range(0, KEEP, 2):
                source = 32 * v + KEEP * (to_lane // SPAN) + j + column // LANES
                pick = (from_row == source).astype(F32).astype(jnp.bfloat16)
                spread = jnp.dot(have, pick, preferred_element_type=F32)
                for k in range(2):
                    here = spread[:, k * LANES:(k + 1) * LANES] == want
                    found = jnp.where(here, base + (32 * v + j + k), found)
            slots[v] = found
            return carry

        lax.fori_loop(0, 4, one, 0)

    def slot(v, t, core_, z_):
        at_ = (t * REPS + core_ * 4 + z_) * 8
        return slots[v, pl.ds(pl.multiple_of(at_, 8), 8), :]

    def spread(values, where):
        return jnp.where(where >= 0, lookup(values, jnp.maximum(where, 0)), 0.0)

    def to_rows(ref, out):
        for t in range(INDEX_TILES * TILES):
            out[4 * t:4 * t + 4, :] = ref[:, t * LANES:(t + 1) * LANES]

    def from_rows(value, relay, ref, c):
        tile, count = CHUNKS[c][:2]
        relay[0:count * BLOCK, :] = value
        for t in range(count * TILES):
            at_ = (tile * TILES + t) * LANES
            ref[:, at_:at_ + LANES] = relay[4 * t:4 * t + 4, :]

    def rows_of(c):
        tile, count = CHUNKS[c][:2]
        return slice(tile * BLOCK, (tile + count) * BLOCK)

    def choose(out, positions, c):
        found = jnp.zeros((8, LANES), F32)
        for t in range(CHUNKS[c][1]):
            places = doubled(positions[t])
            if t % 2:
                places = pltpu.roll(places, 16, 1)
            places = places + SPAN * ((lane // KEEP) % 2)
            for v in range(4):
                mine = lane // 16 == 2 * v + t % 2
                part = out[t * BLOCK + 8 * v:t * BLOCK + 8 * v + 8]
                found = jnp.where(mine, lookup(part, places), found)
        return found

    def transform(c):
        tile, count = CHUNKS[c][:2]
        s2 = buf("s2", c)
        own = DECAY * r_["m_rows"][rows_of(c), :] + s2[zhi]
        r_["blend"][rows_of(c), :] = own
        out = dot(jnp.concatenate([own, s2[1 - zhi]], axis=0), r_["f_v"][...])
        rows = count * BLOCK
        kept[0, zlo, c] = choose(out[:rows], [picks[core, zlo, tile + t] for t in range(count)], c)
        r_["far_kept"][c] = choose(out[rows:], [r_["far_picks"][tile + t] for t in range(count)], c)
        for d, far in ways:
            go(kept_copy(c, d, far))

    def momentum_out(c):
        tile, count = CHUNKS[c][:2]
        z_copy(c).wait_recv()
        now = r_["blend"][rows_of(c), :] + buf("rz", c)[...]
        own = [slot(v, t, core, zlo) for t in range(tile, tile + count) for v in range(4)]
        dense = jnp.where(jnp.concatenate(own, axis=0) >= 0, dot(now, r_["f_v"][...]), 0.0)
        from_rows(now - dot(dense, r_["b_v"][...]), r_["relay0"], r_["nm_out"], c)

    def core_sum(core_, c):
        tile, count = CHUNKS[c][:2]
        parts = []
        for t in range(tile, tile + count):
            for v in range(4):
                total = spread(kept_sum[c, core_, 0], slot(v, t, core_, 0))
                for z_ in range(1, 4):
                    total = total + spread(kept_sum[c, core_, z_], slot(v, t, core_, z_))
                parts.append(total)
        return jnp.concatenate(parts, axis=0)

    def kept_swap(c):
        mine = kept_sum.at[c, core]
        return remote(mine, mine, sems("swap", c, 0), core_partner)

    def kept_add(c):
        kept_end(c)
        kept_sum[c, core] = kept[0, :, c] + kept[1, :, c]
        go(kept_swap(c))

    def params_own(c):
        r_["relay1"][rows_of(c), :] = core_sum(core, c)

    def params_out(c):
        tile, count = CHUNKS[c][:2]
        kept_swap(c).wait_recv()
        average = (r_["relay1"][rows_of(c), :] + core_sum(1 - core, c)) / REPS
        result = r_["p_rows"][rows_of(c), :] - dot(average, r_["b_v"][...])
        from_rows(result, r_["relay2"], r_["np_out"], c)

    loads[0].wait()
    convert(0, 0)
    convert(0, 1)
    pl.semaphore_wait(barrier, len(peers))
    p1_forward(0)
    p1_direct(0)
    loads[1].wait()
    convert(1, 0)
    convert(1, 1)
    p1_forward(1)
    i_start()
    loads[2].wait()
    convert(2, 0)
    convert(2, 1)
    p1_sum(0)
    p1_direct(1)
    p1_forward(2)
    for copy in small[1:]:
        copy.wait()
    to_rows(r_["m_v"], r_["m_rows"])
    to_rows(r_["p_v"], r_["p_rows"])
    p1_sum(1)
    p1_direct(2)
    i_middle()
    p1_end(0)
    p1_sum(2)
    p1_end(1)
    p1_end(2)
    early = len(sent)
    p2_end(0)
    transform(0)
    go(z_copy(0))
    p2_end(1)
    transform(1)
    go(z_copy(1))
    p2_end(2)
    transform(2)
    go(z_copy(2))
    core_copy(picks, "pick", 0).wait_recv()
    make_slots()
    flush(early)
    kept_add(0)
    params_own(0)
    momentum_out(0)
    kept_add(1)
    params_own(1)
    params_out(0)
    momentum_out(1)
    kept_add(2)
    params_own(2)
    params_out(1)
    momentum_out(2)
    params_out(2)
    flush()


def scratches(shape):
    vmem, dma = pltpu.VMEM, pltpu.SemaphoreType.DMA
    made = {
        "m_v": vmem(shape, F32),
        "p_v": vmem(shape, F32),
        "i_v": vmem((4, INDEX_TILES * LANES), jnp.int32),
        "f_v": vmem((LANES, LANES), F32),
        "b_v": vmem((LANES, LANES), F32),
        "m_rows": vmem((INDEX_TILES * BLOCK, LANES), F32),
        "p_rows": vmem((INDEX_TILES * BLOCK, LANES), F32),
        "blend": vmem((INDEX_TILES * BLOCK, LANES), F32),
        "relay0": vmem((INDEX_TILES * BLOCK, LANES), F32),
        "relay2": vmem((INDEX_TILES * BLOCK, LANES), F32),
        "relay1": vmem((INDEX_TILES * BLOCK, LANES), F32),
        "picks": vmem((2, 4, INDEX_TILES, 4, LANES), jnp.int32),
        "slots": vmem((4, INDEX_TILES * REPS * 8, LANES), jnp.int32),
        "kept": vmem((2, 4, len(CHUNKS), 8, LANES), F32),
        "kept_sum": vmem((len(CHUNKS), 2, 4, 8, LANES), F32),
        "far_kept": vmem((len(CHUNKS), 8, LANES), F32),
        "far_picks": vmem((INDEX_TILES, 4, LANES), jnp.int32),
        "spots": vmem((INDEX_TILES * REPS * 8, LANES), F32),
    }
    for c, (_, count, _) in enumerate(CHUNKS):
        block = (count * BLOCK, LANES)
        made["gb" + str(c)] = vmem((128, count * WIDE), jnp.bfloat16)
        made["stage" + str(c)] = vmem((4, 2, 4, *block), F32)
        for name in ("rf", "rd", "rs"):
            made[name + str(c)] = vmem((2, 4, *block), F32)
        made["s1" + str(c)] = vmem((4, 2, *block), F32)
        made["r2" + str(c)] = vmem((3, 2, *block), F32)
        made["s2" + str(c)] = vmem((2, *block), F32)
        made["rz" + str(c)] = vmem(block, F32)
    made["in_sem"] = dma((len(CHUNKS) + 5,))
    for name, count in (("p1", 6), ("p2", 3), ("z", 1), ("pick", 5), ("kept", 7), ("swap", 1)):
        for end in ("_send", "_recv"):
            made[name + end] = dma((len(CHUNKS), count))
    return made


def write(a_ref, b_ref, a_out, b_out, sem):
    copies = [
        pltpu.make_async_copy(a_ref, a_out.at[0], sem.at[0]),
        pltpu.make_async_copy(b_ref, b_out, sem.at[1]),
    ]
    for copy in copies:
        copy.start()
    for copy in copies:
        copy.wait()


def write_out(new_momentum, new_params):
    vmem, hbm = pl.BlockSpec(memory_space=pltpu.VMEM), pl.BlockSpec(memory_space=pltpu.HBM)
    shape = new_params.shape
    return pl.pallas_call(
        write,
        out_shape=(pltpu.HBM((1, *shape), F32), pltpu.HBM(shape, F32)),
        in_specs=[vmem, vmem],
        out_specs=(hbm, hbm),
        scratch_shapes=[pltpu.SemaphoreType.DMA((2,))],
        compiler_params=pltpu.CompilerParams(vmem_limit_bytes=1 << 20),
        name="write",
    )(new_momentum, new_params)


def local(grad_parts, momentum, params, indices):
    forward, back = tables()
    hbm = pl.BlockSpec(memory_space=pltpu.HBM)
    vmem = pl.BlockSpec(memory_space=pltpu.VMEM)
    made = scratches(params.shape)
    names = ("g_hbm", "m_hbm", "p_hbm", "i_hbm", "f_hbm", "b_hbm", "nm_out", "np_out", *made)
    operands = (grad_parts[0, 0], momentum[0], params, indices[0], jnp.asarray(forward), jnp.asarray(back))
    new_momentum, new_params = pl.pallas_call(
        functools.partial(kernel, names),
        out_shape=(pltpu.VMEM(params.shape, F32),) * 2,
        in_specs=[hbm] * 6,
        out_specs=(vmem, vmem),
        scratch_shapes=list(made.values()),
        compiler_params=pltpu.CompilerParams(
            collective_id=0, has_side_effects=True, vmem_limit_bytes=60 << 20
        ),
        name="step",
    )(*(pltpu.with_memory_space_constraint(v, pltpu.HBM) for v in operands))
    return write_out(new_momentum, new_params)


def solution(mesh):
    in_specs = (
        P("rep", "shard", None, None),
        P("rep", "shard", None),
        P("shard", None),
        P("rep", "shard", None),
    )
    out_specs = (P("rep", "shard", None), P("shard", None))
    return jax.shard_map(local, mesh=mesh, in_specs=in_specs, out_specs=out_specs, check_vma=False)
```

```python
import functools
import math

import jax
import jax.numpy as jnp
import numpy as np
from jax import lax
from jax.experimental import pallas as pl
from jax.experimental.pallas import tpu as pltpu
from jax.sharding import PartitionSpec as P

SPAN = 64
KEEP = 8
REPS = 8
DECAY = 0.9
LANES = 128
TILES = 8
BLOCK = 4 * TILES
WIDE = TILES * LANES
CHUNKS = ((4, 1, 0), (0, 2, 1), (2, 2, 0))
INDEX_TILES = 5
MESH = pl.DeviceIdType.MESH
F32 = jnp.float32


def tables():
    freq = np.arange(SPAN, dtype=np.float64)[:, None]
    place = np.arange(SPAN, dtype=np.float64)[None, :]
    table = np.cos(math.pi * (place + 0.5) * freq / SPAN)
    table = table * np.where(freq == 0.0, math.sqrt(1.0 / SPAN), math.sqrt(2.0 / SPAN))
    pair = np.kron(np.eye(2), table)
    return pair.T.astype(np.float32), pair.astype(np.float32)


def dot(a, b):
    return jnp.dot(a, b, precision=lax.Precision.HIGHEST, preferred_element_type=F32)


def lookup(values, lanes):
    return jnp.take_along_axis(values, lanes, axis=1, mode="promise_in_bounds")


def kernel(names, *refs):
    r_ = dict(zip(names, refs))
    rep, shard = lax.axis_index("rep"), lax.axis_index("shard")
    zlo, core = rep // 2, rep % 2
    zhi, y, x = shard // 16, (shard // 4) % 4, shard % 4

    def at(zhi_, y_, x_):
        return (rep, zhi_ * 16 + y_ * 4 + x_)

    def step_x(d):
        return at(zhi, y, (x + d) % 4)

    def step_y(d):
        return at(zhi, (y + d) % 4, x)

    core_partner = (zlo * 2 + 1 - core, shard)

    def step_l(d, far=0):
        half_ = zhi + far * (1 - 2 * zhi)
        return (((zlo + d) % 4) * 2 + core, half_ * 16 + y * 4 + x)

    def swap(c):
        return (core + CHUNKS[c][2]) % 2

    def first(c, d):
        s = swap(c)
        return at(zhi, (y + s * d) % 4, (x + (1 - s) * d) % 4)

    def second(c, d):
        s = swap(c)
        return at(zhi, (y + (1 - s) * d) % 4, (x + s * d) % 4)

    def place_a(c):
        return x + swap(c) * (y - x)

    def place_b(c):
        return y + swap(c) * (x - y)

    def buf(name, c):
        return r_[name + str(c)]

    def sems(name, c, n):
        return r_[name + "_send"].at[c, n], r_[name + "_recv"].at[c, n]

    def remote(src, dst, pair, device):
        return pltpu.make_async_remote_copy(
            src_ref=src, dst_ref=dst, send_sem=pair[0], recv_sem=pair[1],
            device_id=device, device_id_type=MESH,
        )

    sent = []

    def go(copy):
        copy.start()
        sent.append(copy)

    def flush(count=None):
        for copy in sent[:count]:
            copy.wait_send()
        del sent[:count]

    barrier = pltpu.get_barrier_semaphore()
    peers = [step_x(1), step_x(3), step_y(1), step_y(3), step_x(2), step_y(2)]
    peers += [core_partner] + [step_l(d) for d in (1, 2, 3)] + [step_l(d, 1) for d in range(4)]
    for peer in peers:
        pl.semaphore_signal(barrier, inc=1, device_id=peer, device_id_type=MESH)

    loads = []
    for c, (tile, count, _) in enumerate(CHUNKS):
        loads.append(
            pltpu.make_async_copy(
                r_["g_hbm"].at[:, pl.ds(tile * WIDE, count * WIDE)], buf("gb", c), r_["in_sem"].at[c]
            )
        )
    small = [
        pltpu.make_async_copy(r_[a], r_[b], r_["in_sem"].at[len(CHUNKS) + n])
        for n, (a, b) in enumerate(
            (("i_hbm", "i_v"), ("m_hbm", "m_v"), ("p_hbm", "p_v"), ("f_hbm", "f_v"), ("b_hbm", "b_v"))
        )
    ]
    for copy in loads[:1] + small[:1] + loads[1:] + small[1:]:
        copy.start()

    upper = lax.broadcasted_iota(jnp.int32, (8, LANES), 0) // 4
    lane = lax.broadcasted_iota(jnp.int32, (8, LANES), 1)
    low_half = upper == 0

    def convert(c, z_):
        s = swap(c)
        gb, stage = buf("gb", c), buf("stage", c)

        def group(y_, carry):
            rows = pl.ds(pl.multiple_of(z_ * 64 + y_ * 16, 16), 16)
            for t in range(0, CHUNKS[c][1] * TILES, 2):
                one = gb[rows, t * LANES:(t + 1) * LANES].astype(F32)
                two = gb[rows, (t + 1) * LANES:(t + 2) * LANES].astype(F32)
                for h in range(2):
                    u, v = one[8 * h:8 * h + 8], two[8 * h:8 * h + 8]
                    for q in range(2):
                        x_ = 2 * h + q
                        if q == 0:
                            piece = jnp.where(low_half, u, pltpu.roll(v, 4, 0))
                        else:
                            piece = jnp.where(low_half, pltpu.roll(u, 4, 0), v)
                        a_, b_ = x_ + s * (y_ - x_), y_ + s * (x_ - y_)
                        stage[a_, z_, b_, 4 * t:4 * t + 8, :] = piece
            return carry

        lax.fori_loop(0, 4, group, 0)

    def half(c, q, h):
        return buf("stage", c).at[q, h]

    def got(c, kind, h):
        return buf(("rf", "rd", "rs")[kind], c).at[h]

    def p1_copy(c, n, q, h, kind, slot, d):
        return remote(half(c, q, h), got(c, kind, slot), sems("p1", c, n), first(c, d))

    def p1_forward(c):
        far = (place_a(c) + 2) % 4
        go(p1_copy(c, 0, far, 0, 0, 0, 1))
        go(p1_copy(c, 1, far, 1, 0, 1, 3))

    def p1_direct(c):
        p = place_a(c)
        go(p1_copy(c, 2, (p + 1) % 4, 1, 1, 1, 1))
        go(p1_copy(c, 3, (p + 3) % 4, 0, 1, 0, 3))

    def p1_wait(c, n, kind, slot):
        p1_copy(c, n, place_a(c), slot, kind, slot, 1).wait_recv()

    def p1_sum(c):
        p = place_a(c)
        up, down = (p + 1) % 4, (p + 3) % 4
        p1_wait(c, 0, 0, 0)
        half(c, up, 0)[...] += got(c, 0, 0)[...]
        go(p1_copy(c, 4, up, 0, 2, 0, 1))
        p1_wait(c, 1, 0, 1)
        half(c, down, 1)[...] += got(c, 0, 1)[...]
        go(p1_copy(c, 5, down, 1, 2, 1, 3))

    def p2_copy(c, q, d):
        return remote(buf("s1", c).at[q], buf("r2", c).at[d - 1], sems("p2", c, d - 1), second(c, d))

    def p1_end(c):
        p, s1 = place_a(c), buf("s1", c)
        for n, kind, slot in ((3, 1, 0), (2, 1, 1), (4, 2, 0), (5, 2, 1)):
            p1_wait(c, n, kind, slot)
        for h in range(2):
            own, direct, summed = half(c, p, h), got(c, 1, h), got(c, 2, h)
            for n in range(4):
                s1[n, h] = own[n] + direct[n] + summed[n]
        q = place_b(c)
        for d in (2, 1, 3):
            go(p2_copy(c, (q + d) % 4, d))

    def z_copy(c):
        return remote(buf("s2", c).at[1 - zhi], buf("rz", c), sems("z", c, 0), step_l(0, 1))

    def p2_end(c):
        q, r2 = place_b(c), buf("r2", c)
        for d in (1, 3, 2):
            p2_copy(c, q, d).wait_recv()
        buf("s2", c)[...] = buf("s1", c)[q] + r2[0] + r2[1] + r2[2]

    def pick_copy(d):
        mine = r_["picks"].at[core, zlo]
        return remote(mine, mine, sems("pick", 0, d), step_l(d))

    def pick_far():
        return remote(r_["picks"].at[core, zlo], r_["far_picks"], sems("pick", 0, 4), step_l(0, 1))

    def core_copy(ref, name, n):
        return remote(ref.at[core], ref.at[core], sems(name, 0, n), core_partner)

    def kept_copy(c, d, far):
        source = r_["far_kept"].at[c] if far else r_["kept"].at[0, zlo, c]
        n = 3 + d if far else d - 1
        return remote(source, r_["kept"].at[far, zlo, c], sems("kept", c, n), step_l(d, far))

    ways = ((0, 1), (2, 0), (1, 1), (3, 1), (1, 0), (3, 0), (2, 1))

    def kept_end(c):
        for d, far in ways:
            kept_copy(c, d, far).wait_recv()

    picks, slots, spots, kept, kept_sum = r_["picks"], r_["slots"], r_["spots"], r_["kept"], r_["kept_sum"]

    def i_start():
        small[0].wait()
        for t in range(INDEX_TILES):
            picks[core, zlo, t] = r_["i_v"][:, t * LANES:(t + 1) * LANES]
        for d in (2, 1, 3):
            go(pick_copy(d))
        go(pick_far())

    def i_middle():
        for d in (1, 3, 2):
            pick_copy(d).wait_recv()
        go(core_copy(picks, "pick", 0))
        pick_far().wait_recv()

    def doubled(four):
        return jnp.concatenate([four, pltpu.roll(four, LANES - 16, 1)], axis=0)

    def make_slots():
        rows = INDEX_TILES * REPS * 8
        for t in range(INDEX_TILES):
            for r in range(REPS):
                at_ = (t * REPS + r) * 8
                spots[at_:at_ + 8, :] = doubled(picks[r // 4, r % 4, t]).astype(F32)
        from_row = lax.broadcasted_iota(jnp.int32, (LANES, 2 * LANES), 0)
        column = lax.broadcasted_iota(jnp.int32, (LANES, 2 * LANES), 1)
        to_lane = column % LANES
        wide = lax.broadcasted_iota(jnp.int32, (rows, LANES), 1)
        want = (wide % SPAN).astype(F32)
        tile_of = lax.broadcasted_iota(jnp.int32, (rows, LANES), 0) // (REPS * 8)
        base = KEEP * (wide // SPAN) + 16 * (tile_of % 2)
        have = spots[...].astype(jnp.bfloat16)

        def one(v, carry):
            found = jnp.full((rows, LANES), -1, jnp.int32)
            for j in range(0, KEEP, 2):
                source = 32 * v + KEEP * (to_lane // SPAN) + j + column // LANES
                pick = (from_row == source).astype(F32).astype(jnp.bfloat16)
                spread = jnp.dot(have, pick, preferred_element_type=F32)
                for k in range(2):
                    here = spread[:, k * LANES:(k + 1) * LANES] == want
                    found = jnp.where(here, base + (32 * v + j + k), found)
            slots[v] = found
            return carry

        lax.fori_loop(0, 4, one, 0)

    def slot(v, t, core_, z_):
        at_ = (t * REPS + core_ * 4 + z_) * 8
        return slots[v, pl.ds(pl.multiple_of(at_, 8), 8), :]

    def spread(values, where):
        return jnp.where(where >= 0, lookup(values, jnp.maximum(where, 0)), 0.0)

    def to_rows(ref, out):
        for t in range(INDEX_TILES * TILES):
            out[4 * t:4 * t + 4, :] = ref[:, t * LANES:(t + 1) * LANES]

    def from_rows(value, relay, ref, c):
        tile, count = CHUNKS[c][:2]
        relay[0:count * BLOCK, :] = value
        for t in range(count * TILES):
            at_ = (tile * TILES + t) * LANES
            ref[:, at_:at_ + LANES] = relay[4 * t:4 * t + 4, :]

    def rows_of(c):
        tile, count = CHUNKS[c][:2]
        return slice(tile * BLOCK, (tile + count) * BLOCK)

    def choose(out, positions, c):
        found = jnp.zeros((8, LANES), F32)
        for t in range(CHUNKS[c][1]):
            places = doubled(positions[t])
            if t % 2:
                places = pltpu.roll(places, 16, 1)
            places = places + SPAN * ((lane // KEEP) % 2)
            for v in range(4):
                mine = lane // 16 == 2 * v + t % 2
                part = out[t * BLOCK + 8 * v:t * BLOCK + 8 * v + 8]
                found = jnp.where(mine, lookup(part, places), found)
        return found

    def transform(c):
        tile, count = CHUNKS[c][:2]
        s2 = buf("s2", c)
        own = DECAY * r_["m_rows"][rows_of(c), :] + s2[zhi]
        r_["blend"][rows_of(c), :] = own
        out = dot(jnp.concatenate([own, s2[1 - zhi]], axis=0), r_["f_v"][...])
        rows = count * BLOCK
        kept[0, zlo, c] = choose(out[:rows], [picks[core, zlo, tile + t] for t in range(count)], c)
        r_["far_kept"][c] = choose(out[rows:], [r_["far_picks"][tile + t] for t in range(count)], c)
        for d, far in ways:
            go(kept_copy(c, d, far))

    def momentum_out(c):
        tile, count = CHUNKS[c][:2]
        z_copy(c).wait_recv()
        now = r_["blend"][rows_of(c), :] + buf("rz", c)[...]
        own = [slot(v, t, core, zlo) for t in range(tile, tile + count) for v in range(4)]
        dense = jnp.where(jnp.concatenate(own, axis=0) >= 0, dot(now, r_["f_v"][...]), 0.0)
        from_rows(now - dot(dense, r_["b_v"][...]), r_["relay0"], r_["nm_out"], c)

    def core_sum(core_, c):
        tile, count = CHUNKS[c][:2]
        parts = []
        for t in range(tile, tile + count):
            for v in range(4):
                total = spread(kept_sum[c, core_, 0], slot(v, t, core_, 0))
                for z_ in range(1, 4):
                    total = total + spread(kept_sum[c, core_, z_], slot(v, t, core_, z_))
                parts.append(total)
        return jnp.concatenate(parts, axis=0)

    def kept_swap(c):
        mine = kept_sum.at[c, core]
        return remote(mine, mine, sems("swap", c, 0), core_partner)

    def kept_add(c):
        kept_end(c)
        kept_sum[c, core] = kept[0, :, c] + kept[1, :, c]
        go(kept_swap(c))

    def params_own(c):
        r_["relay1"][rows_of(c), :] = core_sum(core, c)

    def params_out(c):
        tile, count = CHUNKS[c][:2]
        kept_swap(c).wait_recv()
        average = (r_["relay1"][rows_of(c), :] + core_sum(1 - core, c)) / REPS
        result = r_["p_rows"][rows_of(c), :] - dot(average, r_["b_v"][...])
        from_rows(result, r_["relay2"], r_["np_out"], c)

    loads[0].wait()
    convert(0, 0)
    convert(0, 1)
    pl.semaphore_wait(barrier, len(peers))
    p1_forward(0)
    p1_direct(0)
    loads[1].wait()
    convert(1, 0)
    convert(1, 1)
    p1_forward(1)
    i_start()
    loads[2].wait()
    convert(2, 0)
    convert(2, 1)
    p1_sum(0)
    p1_direct(1)
    p1_forward(2)
    for copy in small[1:]:
        copy.wait()
    to_rows(r_["m_v"], r_["m_rows"])
    to_rows(r_["p_v"], r_["p_rows"])
    p1_sum(1)
    p1_direct(2)
    i_middle()
    p1_end(0)
    p1_sum(2)
    p1_end(1)
    p1_end(2)
    early = len(sent)
    p2_end(0)
    transform(0)
    go(z_copy(0))
    p2_end(1)
    transform(1)
    go(z_copy(1))
    p2_end(2)
    transform(2)
    go(z_copy(2))
    core_copy(picks, "pick", 0).wait_recv()
    make_slots()
    flush(early)
    kept_add(0)
    params_own(0)
    momentum_out(0)
    kept_add(1)
    params_own(1)
    params_out(0)
    momentum_out(1)
    kept_add(2)
    params_own(2)
    params_out(1)
    momentum_out(2)
    params_out(2)
    flush()


def scratches(shape):
    vmem, dma = pltpu.VMEM, pltpu.SemaphoreType.DMA
    made = {
        "m_v": vmem(shape, F32),
        "p_v": vmem(shape, F32),
        "i_v": vmem((4, INDEX_TILES * LANES), jnp.int32),
        "f_v": vmem((LANES, LANES), F32),
        "b_v": vmem((LANES, LANES), F32),
        "m_rows": vmem((INDEX_TILES * BLOCK, LANES), F32),
        "p_rows": vmem((INDEX_TILES * BLOCK, LANES), F32),
        "blend": vmem((INDEX_TILES * BLOCK, LANES), F32),
        "relay0": vmem((INDEX_TILES * BLOCK, LANES), F32),
        "relay2": vmem((INDEX_TILES * BLOCK, LANES), F32),
        "relay1": vmem((INDEX_TILES * BLOCK, LANES), F32),
        "picks": vmem((2, 4, INDEX_TILES, 4, LANES), jnp.int32),
        "slots": vmem((4, INDEX_TILES * REPS * 8, LANES), jnp.int32),
        "kept": vmem((2, 4, len(CHUNKS), 8, LANES), F32),
        "kept_sum": vmem((len(CHUNKS), 2, 4, 8, LANES), F32),
        "far_kept": vmem((len(CHUNKS), 8, LANES), F32),
        "far_picks": vmem((INDEX_TILES, 4, LANES), jnp.int32),
        "spots": vmem((INDEX_TILES * REPS * 8, LANES), F32),
    }
    for c, (_, count, _) in enumerate(CHUNKS):
        block = (count * BLOCK, LANES)
        made["gb" + str(c)] = vmem((128, count * WIDE), jnp.bfloat16)
        made["stage" + str(c)] = vmem((4, 2, 4, *block), F32)
        for name in ("rf", "rd", "rs"):
            made[name + str(c)] = vmem((2, 4, *block), F32)
        made["s1" + str(c)] = vmem((4, 2, *block), F32)
        made["r2" + str(c)] = vmem((3, 2, *block), F32)
        made["s2" + str(c)] = vmem((2, *block), F32)
        made["rz" + str(c)] = vmem(block, F32)
    made["in_sem"] = dma((len(CHUNKS) + 5,))
    for name, count in (("p1", 6), ("p2", 3), ("z", 1), ("pick", 5), ("kept", 7), ("swap", 1)):
        for end in ("_send", "_recv"):
            made[name + end] = dma((len(CHUNKS), count))
    return made


def write(a_ref, b_ref, a_out, b_out, sem):
    copies = [
        pltpu.make_async_copy(a_ref, a_out.at[0], sem.at[0]),
        pltpu.make_async_copy(b_ref, b_out, sem.at[1]),
    ]
    for copy in copies:
        copy.start()
    for copy in copies:
        copy.wait()


def write_out(new_momentum, new_params):
    vmem, hbm = pl.BlockSpec(memory_space=pltpu.VMEM), pl.BlockSpec(memory_space=pltpu.HBM)
    shape = new_params.shape
    return pl.pallas_call(
        write,
        out_shape=(pltpu.HBM((1, *shape), F32), pltpu.HBM(shape, F32)),
        in_specs=[vmem, vmem],
        out_specs=(hbm, hbm),
        scratch_shapes=[pltpu.SemaphoreType.DMA((2,))],
        compiler_params=pltpu.CompilerParams(vmem_limit_bytes=1 << 20),
        name="write",
    )(new_momentum, new_params)


def local(grad_parts, momentum, params, indices):
    forward, back = tables()
    hbm = pl.BlockSpec(memory_space=pltpu.HBM)
    vmem = pl.BlockSpec(memory_space=pltpu.VMEM)
    made = scratches(params.shape)
    names = ("g_hbm", "m_hbm", "p_hbm", "i_hbm", "f_hbm", "b_hbm", "nm_out", "np_out", *made)
    operands = (grad_parts[0, 0], momentum[0], params, indices[0], jnp.asarray(forward), jnp.asarray(back))
    new_momentum, new_params = pl.pallas_call(
        functools.partial(kernel, names),
        out_shape=(pltpu.VMEM(params.shape, F32),) * 2,
        in_specs=[hbm] * 6,
        out_specs=(vmem, vmem),
        scratch_shapes=list(made.values()),
        compiler_params=pltpu.CompilerParams(
            collective_id=0, has_side_effects=True, vmem_limit_bytes=60 << 20
        ),
        name="step",
    )(*(pltpu.with_memory_space_constraint(v, pltpu.HBM) for v in operands))
    return write_out(new_momentum, new_params)


def solution(mesh):
    in_specs = (
        P("rep", "shard", None, None),
        P("rep", "shard", None),
        P("shard", None),
        P("rep", "shard", None),
    )
    out_specs = (P("rep", "shard", None), P("shard", None))
    return jax.shard_map(local, mesh=mesh, in_specs=in_specs, out_specs=out_specs, check_vma=False)
```
